256 devices in a mesh: dp: 16 (over z, y_lo), mp: 16 (over x, y_hi, core).
Axes of the slice: x: 4, y: 4 (y_hi: 2, y_lo: 2; y = y_hi * 2 + y_lo), z: 8, core: 2. Of those that a mesh axis runs over, the one named last changes fastest.
Arguments:
- query_acts: bfloat16 [16, 32, 4096], P('dp', None, 'mp'), may hold values from -6 to 6
- query_grads: bfloat16 [16, 32, 28672], P('dp', None, 'mp'), may hold values from -6 to 6
- train_acts: bfloat16 [16, 32, 4096], P('dp', None, 'mp'), may hold values from -6 to 6
- train_grads: bfloat16 [16, 32, 28672], P('dp', None, 'mp'), may hold values from -6 to 6
- basis_in: bfloat16 [4096, 4096], P('dp', 'mp'), may hold values from -0.09375 to 0.09375
- basis_out: bfloat16 [28672, 28672], P('mp', 'dp'), may hold values from -0.03125 to 0.03125
- eigen: float32 [28672, 4096], P('dp', 'mp'), may hold values from 0.05 to 2
Outputs:
- scores: float32 [16, 16], replicated
The draws below stay inside these ranges and needn't reach their ends.
All inputs are finite; a program needn't handle non-finite values.
Results may differ from the reference program's by a relative error of at most 0.0049.
Values may be sent and summed in bfloat16 or wider, within the bound.
No kernel may reach another device: no remote copies, remote signals or barrier semaphores. Data moves between devices by JAX's collectives and lax.ppermute only.
A program may use at most 128 MiB of HBM per device.

```python
import math
import jax
import jax.numpy as jnp
from jax import lax

IN = 4096
OUT = 28672
TS = 32
TQ = 32
NQ = 16
NS = 16


def shard_levels(rng, dims, pieces, low, high):
    gain, own = 1.0, jax.random.fold_in(rng, 6)
    for position, blocks in pieces:
        steps = jnp.exp(jax.random.uniform(jax.random.fold_in(own, position), (blocks,), jnp.float32, low / len(pieces), high / len(pieces)))
        gain = gain * jnp.repeat(steps, dims[position] // blocks).reshape([-1 if axis == position else 1 for axis in range(len(dims))])
    return gain


def scatter_about(own_key, extent, deviation, limit, cuts=(), kind=jnp.bfloat16):
    gain = shard_levels(own_key, extent, cuts, -0.22, 0.18) if cuts else 1.0
    drawn = jax.random.normal(own_key, extent, jnp.float32) * deviation * gain
    return jnp.minimum(jnp.maximum(drawn, -limit), limit).astype(kind)


def setup_inputs(seed: int = 0) -> dict:
    keys = jax.random.split(jax.random.key(seed), 8)
    query_acts = scatter_about(keys[0], (NQ, TQ, IN), 1.0, 6.0, ((0, 16), (2, 16)))
    query_grads = scatter_about(keys[1], (NQ, TQ, OUT), 1.0, 6.0, ((0, 16), (2, 16)))
    train_acts = scatter_about(keys[2], (NS, TS, IN), 1.0, 6.0, ((0, 16), (2, 16)))
    train_grads = scatter_about(keys[3], (NS, TS, OUT), 1.0, 6.0, ((0, 16), (2, 16)))
    basis_in = scatter_about(keys[4], (IN, IN), IN ** -0.5, 0.09375, ((0, 16), (1, 16)))
    basis_out = scatter_about(keys[5], (OUT, OUT), OUT ** -0.5, 0.03125, ((0, 16), (1, 16)))
    eigen = jnp.clip(jnp.exp(math.log(2.0) - 3.6888794 * jax.random.uniform(keys[6], (OUT, IN), jnp.float32) ** shard_levels(keys[6], (OUT, IN), ((0, 16), (1, 16)), -0.2, 0.2)), 0.05, 2.0)
    return dict(query_acts=query_acts, query_grads=query_grads, train_acts=train_acts, train_grads=train_grads, basis_in=basis_in, basis_out=basis_out, eigen=eigen)


damping = 0.1


def rotate(tokens, basis):
    flat = tokens.reshape(tokens.shape[0] * tokens.shape[1], tokens.shape[2])
    turned = jnp.dot(flat, basis, preferred_element_type=jnp.float32).astype(jnp.bfloat16)
    return turned.reshape(tokens.shape[0], tokens.shape[1], basis.shape[1])


def reference(query_acts, query_grads, train_acts, train_grads, basis_in, basis_out, eigen):
    rot_query_acts = rotate(query_acts, basis_in).astype(jnp.float32)
    rot_train_acts = rotate(train_acts, basis_in).astype(jnp.float32)
    rot_query_grads = rotate(query_grads, basis_out)
    rot_train_grads = rotate(train_grads, basis_out)
    block_width = OUT // 16
    normalizer = float(TQ * TS * IN * OUT) ** -0.5

    def one_block(running, block_index):
        offset = block_index * block_width
        query_part = lax.dynamic_slice_in_dim(rot_query_grads, offset, block_width, 2).astype(jnp.float32)
        train_part = lax.dynamic_slice_in_dim(rot_train_grads, offset, block_width, 2).astype(jnp.float32)
        eigen_rows = lax.dynamic_slice_in_dim(eigen, offset, block_width, 0)
        query_gradient = jnp.einsum('ntd,nte->nde', query_part, rot_query_acts)
        preconditioned = (query_gradient / (eigen_rows + damping)).astype(jnp.bfloat16)
        preconditioned = lax.optimization_barrier(preconditioned).astype(jnp.float32)
        train_gradient = jnp.einsum('std,ste->sde', train_part, rot_train_acts).astype(jnp.bfloat16)
        train_gradient = lax.optimization_barrier(train_gradient).astype(jnp.float32)
        return running + jnp.einsum('nde,sde->ns', preconditioned, train_gradient), None

    initial = jnp.zeros((query_acts.shape[0], train_acts.shape[0]), jnp.float32)
    summed, _ = lax.scan(one_block, initial, jnp.arange(16, dtype=jnp.int32))
    return summed * normalizer
```

```python
import jax
import jax.numpy as jnp
from jax import lax
from jax.experimental import pallas as pl
from jax.experimental.pallas import tpu as pltpu
from jax.sharding import PartitionSpec as P

IN = 4096
OUT = 28672
TS = 32
TQ = 32

damping = 0.1

NZ, NYL, NX, NYH, NC = 8, 2, 4, 2, 2
GROUPS = NZ * NYL
CHIPS = NX * NYH


def dp_index(z, yl):
    return (z % NZ) * NYL + yl % NYL


def mp_index(x, yh, core):
    return ((x % NX) * NYH + yh % NYH) * NC + core % NC


def dp_shift(dz, dyl):
    return [
        (dp_index(z, y), dp_index(z + dz, y + dyl)) for z in range(NZ) for y in range(NYL)
    ]


CORE_SWAP = [
    (mp_index(x, h, c), mp_index(x, h, c + 1))
    for x in range(NX)
    for h in range(NYH)
    for c in range(NC)
]
TRANSPOSE = [(d * 16 + m, m * 16 + d) for d in range(16) for m in range(16)]
SAME_CORE = [
    [mp_index(x, h, c) for x in range(NX) for h in range(NYH)] for c in range(NC)
]

CHUNKS = (((0, 0), (0, 1), (1, 0), (-1, 0), (1, 1), (-1, 1),
           (2, 0), (-2, 0), (2, 1), (-2, 1), (3, 0), (-3, 0), (3, 1), (-3, 1), (4, 0), (4, 1)),)


def exchange(x, axis, **kw):
    return lax.all_to_all(x, axis, 0, 0, tiled=True, **kw)


def share(x, count, axis, **kw):
    return exchange(jnp.tile(x, (count, 1)), axis, **kw)


def ring_gather(own):
    held = {(0, 0): own}
    up = down = own
    for k in (1, 2, 3):
        up = lax.ppermute(up, "dp", dp_shift(-1, 0))
        down = lax.ppermute(down, "dp", dp_shift(1, 0))
        held[(k, 0)], held[(-k, 0)] = up, down
    half = own.shape[0] // 2
    held[(4, 0)] = jnp.concatenate(
        [
            lax.ppermute(up[:half], "dp", dp_shift(-1, 0)),
            lax.ppermute(down[half:], "dp", dp_shift(1, 0)),
        ],
        0,
    )
    across = dp_shift(0, 1)
    held[(0, 1)] = lax.ppermute(own, "dp", across)
    for k in (1, 2, 3):
        pair = lax.ppermute(
            jnp.concatenate([held[(k, 0)], held[(-k, 0)]], 0), "dp", across
        )
        held[(k, 1)], held[(-k, 1)] = pair[: own.shape[0]], pair[own.shape[0] :]
    held[(4, 1)] = lax.ppermute(held[(4, 0)], "dp", across)
    return held


def score_kernel(order_ref, place_ref, grads_ref, own_acts_ref, sib_acts_ref, own_inv_ref,
                 sib_inv_ref, out_ref, train_grads, query_acts, train_acts, sums):
    half = own_acts_ref.shape[1]
    rows = 2 * TQ
    for r in range(GROUPS):
        train_grads[r * TS : (r + 1) * TS, :] = grads_ref[r * rows + TQ : (r + 1) * rows, :]
        start = pl.multiple_of(order_ref[r] * rows, rows)
        middle = pl.multiple_of(start + TQ, TQ)
        for ref, at in ((own_acts_ref, 0), (sib_acts_ref, half)):
            query_acts[r * TQ : (r + 1) * TQ, at : at + half] = ref[pl.ds(start, TQ), :]
            train_acts[r * TS : (r + 1) * TS, at : at + half] = ref[
                pl.ds(middle, TS), :
            ].astype(jnp.float32)

    def one_query(n, carry):
        grads = grads_ref[pl.ds(pl.multiple_of(n * rows, rows), TQ), :]
        total = jnp.zeros((GROUPS, 128), jnp.float32)
        for at, inv_ref in ((0, own_inv_ref), (half, sib_inv_ref)):
            acts = query_acts[pl.ds(pl.multiple_of(n * TQ, TQ), TQ), at : at + half]
            gradient = lax.dot_general(
                grads, acts, (((0,), (0,)), ((), ())), preferred_element_type=jnp.float32
            )
            preconditioned = (gradient * inv_ref[...]).astype(jnp.bfloat16)
            projected = jnp.dot(
                train_grads[...], preconditioned, preferred_element_type=jnp.float32
            )
            terms = projected * train_acts[:, at : at + half]
            terms = terms.reshape(GROUPS, TS, half).sum(1)
            for lane in range(0, half, 128):
                total = total + terms[:, lane : lane + 128]
        sums[pl.ds(n, 1)] = total[None]
        return carry

    lax.fori_loop(0, GROUPS, one_query, 0)
    scores = jnp.sum(sums[...], axis=2)
    hot = place_ref[...]
    hot_t = jnp.transpose(hot)
    scores = jnp.dot(
        hot, jnp.dot(scores, hot_t, precision=lax.Precision.HIGHEST),
        precision=lax.Precision.HIGHEST,
    )
    out_ref[...] = jnp.concatenate(
        [scores, jnp.zeros((GROUPS, 128 - GROUPS), jnp.float32)], 1
    )


def score_blocks(order, place, grads, own_acts, sib_acts, own_inv, sib_inv):
    units, half = own_inv.shape
    vmem = pl.BlockSpec(memory_space=pltpu.VMEM)
    return pl.pallas_call(
        score_kernel,
        out_shape=jax.ShapeDtypeStruct((GROUPS, 128), jnp.float32),
        in_specs=[pl.BlockSpec(memory_space=pltpu.SMEM)] + [vmem] * 6,
        out_specs=vmem,
        scratch_shapes=[
            pltpu.VMEM((GROUPS * TS, units), jnp.bfloat16),
            pltpu.VMEM((GROUPS * TQ, 2 * half), jnp.bfloat16),
            pltpu.VMEM((GROUPS * TS, 2 * half), jnp.float32),
            pltpu.VMEM((GROUPS, GROUPS, 128), jnp.float32),
        ],
        compiler_params=pltpu.CompilerParams(vmem_limit_bytes=40 * 1024 * 1024),
        cost_estimate=pl.CostEstimate(
            flops=2 * GROUPS * units * 2 * half * (GROUPS * TS + TQ),
            bytes_accessed=8 * 1024 * 1024,
            transcendentals=0,
        ),
    )(order, place, grads, own_acts, sib_acts, own_inv, sib_inv)


def shards(query_acts, query_grads, train_acts, train_grads, basis_in, basis_out, eigen):
    in_local = query_acts.shape[2]
    out_local = query_grads.shape[2]
    rows = 2 * TQ
    acts = jnp.concatenate(
        [query_acts.reshape(TQ, in_local), train_acts.reshape(TS, in_local)], 0
    )
    grads = jnp.concatenate(
        [query_grads.reshape(TQ, out_local), train_grads.reshape(TS, out_local)], 0
    )
    dp = lax.axis_index("dp")
    core = lax.axis_index("mp") % NC
    half = out_local // 2
    own_at, sib_at = core * half, (1 - core) * half

    own_inv = 1.0 / (lax.dynamic_slice_in_dim(eigen, own_at, half, 0) + damping)
    sib_inv = 1.0 / (
        lax.ppermute(lax.dynamic_slice_in_dim(eigen, sib_at, half, 0), "mp", CORE_SWAP) + damping
    )
    own_basis = lax.dynamic_slice_in_dim(basis_out, own_at, half, 1)
    sib_basis = lax.dynamic_slice_in_dim(basis_out, sib_at, half, 1)

    moved = lax.ppermute(acts, ("dp", "mp"), TRANSPOSE)
    all_acts = share(moved, GROUPS, "mp")
    part_acts = jnp.dot(all_acts, basis_in, preferred_element_type=jnp.float32)
    own_rows = exchange(part_acts, "dp").reshape(GROUPS, rows, in_local).sum(0)
    own_acts = share(own_rows.astype(jnp.bfloat16), GROUPS, "dp")
    sib_acts = lax.ppermute(own_acts, "mp", CORE_SWAP)

    held = ring_gather(grads)
    turned = []
    for chunk in CHUNKS:
        tokens = jnp.concatenate([held[place] for place in chunk], 0)
        sib_part = jnp.dot(tokens, sib_basis, preferred_element_type=jnp.float32)
        got = lax.ppermute(sib_part.astype(jnp.bfloat16), "mp", CORE_SWAP)
        own_part = jnp.dot(tokens, own_basis, preferred_element_type=jnp.float32)
        pair = (own_part + got.astype(jnp.float32)).astype(jnp.bfloat16)
        parts = exchange(pair, "mp", axis_index_groups=SAME_CORE)
        summed = parts.reshape(CHIPS, -1, half).astype(jnp.float32).sum(0)
        turned.append(
            share(summed.astype(jnp.bfloat16), CHIPS, "mp", axis_index_groups=SAME_CORE)
        )
    all_grads = jnp.concatenate(turned, 0)

    places = [place for chunk in CHUNKS for place in chunk]
    dz = jnp.array([p[0] for p in places], jnp.int32)
    dy = jnp.array([p[1] for p in places], jnp.int32)
    order = ((dp // NYL + dz + NZ) % NZ) * NYL + (dp % NYL + dy) % NYL
    place = (order[None, :] == jnp.arange(GROUPS, dtype=jnp.int32)[:, None]).astype(jnp.float32)

    scores = score_blocks(order, place, all_grads, own_acts, sib_acts, own_inv, sib_inv)
    normalizer = float(TQ * TS * IN * OUT) ** (-0.5)
    scores = share(scores * normalizer, GROUPS, "mp").reshape(GROUPS, GROUPS, 128).sum(0)
    scores = share(scores, GROUPS, "dp").reshape(GROUPS, GROUPS, 128).sum(0)
    return scores[:, :GROUPS]


def solution(mesh):
    placed = (
        P("dp", None, "mp"),
        P("dp", None, "mp"),
        P("dp", None, "mp"),
        P("dp", None, "mp"),
        P("dp", "mp"),
        P("mp", "dp"),
        P("dp", "mp"),
    )
    return jax.shard_map(shards, mesh=mesh, in_specs=placed, out_specs=P(), check_vma=False)
```

```python
import functools

import jax
import jax.numpy as jnp
from jax import lax
from jax.experimental import pallas as pl
from jax.experimental.pallas import tpu as pltpu
from jax.sharding import PartitionSpec as P

IN = 4096
OUT = 28672
TS = 32
TQ = 32

damping = 0.1

NZ, NYL, NX, NYH, NC = 8, 2, 4, 2, 2
GROUPS = NZ * NYL
CHIPS = NX * NYH


def dp_index(z, yl):
    return (z % NZ) * NYL + yl % NYL


def mp_index(x, yh, core):
    return ((x % NX) * NYH + yh % NYH) * NC + core % NC


def dp_shift(dz, dyl):
    return [
        (dp_index(z, y), dp_index(z + dz, y + dyl)) for z in range(NZ) for y in range(NYL)
    ]


CORE_SWAP = [
    (mp_index(x, h, c), mp_index(x, h, c + 1))
    for x in range(NX)
    for h in range(NYH)
    for c in range(NC)
]
TRANSPOSE = [(d * 16 + m, m * 16 + d) for d in range(16) for m in range(16)]
CHIP_TRANSPOSE = [
    ((z * NYL + yl) * 16 + q * NC + c, (q * NYL + yl) * 16 + z * NC + c)
    for z in range(NZ)
    for yl in range(NYL)
    for q in range(NX * NYH)
    for c in range(NC)
]
SAME_CORE = [
    [mp_index(x, h, c) for x in range(NX) for h in range(NYH)] for c in range(NC)
]

CHUNKS = (
    ((0, 0), (0, 1), (1, 0), (-1, 0), (1, 1), (-1, 1), (2, 0), (2, 1)),
    ((-2, 0), (-2, 1), (3, 0), (-3, 0), (3, 1), (-3, 1), (4, 0), (4, 1)),
)
RING = (0, 1, -1, 2, -2, 3, -3, 4)


def exchange(x, axis, **kw):
    return lax.all_to_all(x, axis, 0, 0, tiled=True, **kw)


def share(x, count, axis, **kw):
    return exchange(jnp.tile(x, (count, 1)), axis, **kw)


def z_ring(own):
    held = {0: own}
    up = down = own
    for k in (1, 2, 3):
        up = lax.ppermute(up, "dp", dp_shift(-1, 0))
        down = lax.ppermute(down, "dp", dp_shift(1, 0))
        held[k], held[-k] = up, down
    half = own.shape[0] // 2
    held[4] = jnp.concatenate(
        [
            lax.ppermute(up[:half], "dp", dp_shift(-1, 0)),
            lax.ppermute(down[half:], "dp", dp_shift(1, 0)),
        ],
        0,
    )
    return held


def ring_gather(own):
    along = z_ring(own)
    held = {(k, 0): block for k, block in along.items()}
    across = dp_shift(0, 1)
    rows = own.shape[0]
    held[(0, 1)] = lax.ppermute(own, "dp", across)
    for k in (1, 2, 3):
        pair = lax.ppermute(jnp.concatenate([along[k], along[-k]], 0), "dp", across)
        held[(k, 1)], held[(-k, 1)] = pair[:rows], pair[rows:]
    held[(4, 1)] = lax.ppermute(along[4], "dp", across)
    return held


def turn_kernel(count, core_ref, *refs):
    del core_ref
    blocks = refs[:count]
    out_basis, in_basis, sib_ref, own_ref, tokens = refs[count:]
    rows = blocks[0].shape[0]
    features, units = out_basis.shape
    step = pl.program_id(0)

    @pl.when(step == 0)
    def _():
        for r, ref in enumerate(blocks):
            tokens[r * rows : (r + 1) * rows, :] = ref[...]

    def products():
        grads = jnp.dot(
            tokens[:, :features], out_basis[...], preferred_element_type=jnp.float32
        )
        acts = jnp.dot(
            tokens[:, features:], in_basis[...], preferred_element_type=jnp.float32
        )
        return grads, acts

    @pl.when(step == 0)
    def _():
        grads, acts = products()
        high = acts.astype(jnp.bfloat16)
        sib_ref[:, :units] = grads.astype(jnp.bfloat16)
        sib_ref[:, units : units + 128] = high
        sib_ref[:, units + 128 :] = (acts - high.astype(jnp.float32)).astype(jnp.bfloat16)

    @pl.when(step == 1)
    def _():
        grads, acts = products()
        own_ref[:, :units] = grads
        own_ref[:, units:] = acts


def turn(core, blocks, basis_out, basis_in):
    rows, width = blocks[0].shape
    features, units = basis_out.shape[0], basis_out.shape[1] // 2
    tokens = rows * len(blocks)
    whole = lambda i, core_ref: (0, 0)
    side = lambda i, core_ref: (0, jnp.where(i == 0, 1 - core_ref[0], core_ref[0]))
    return pl.pallas_call(
        functools.partial(turn_kernel, len(blocks)),
        grid_spec=pltpu.PrefetchScalarGridSpec(
            num_scalar_prefetch=1,
            grid=(2,),
            in_specs=[pl.BlockSpec((rows, width), whole)] * len(blocks)
            + [
                pl.BlockSpec((features, units), side),
                pl.BlockSpec((width - features, 128), side),
            ],
            out_specs=[
                pl.BlockSpec((tokens, units + 256), whole),
                pl.BlockSpec((tokens, units + 128), whole),
            ],
            scratch_shapes=[pltpu.VMEM((tokens, width), jnp.bfloat16)],
        ),
        out_shape=[
            jax.ShapeDtypeStruct((tokens, units + 256), jnp.bfloat16),
            jax.ShapeDtypeStruct((tokens, units + 128), jnp.float32),
        ],
        compiler_params=pltpu.CompilerParams(vmem_limit_bytes=32 * 1024 * 1024),
        cost_estimate=pl.CostEstimate(
            flops=2 * tokens * (features + 256) * (units + 128) * 2,
            bytes_accessed=2 * tokens * (width + 3 * units) + 4 * features * units,
            transcendentals=0,
        ),
    )(core.reshape(1), *blocks, basis_out, basis_in)


def pair_kernel(own_ref, got_ref, out_ref):
    units = own_ref.shape[1] - 128
    got = got_ref[...].astype(jnp.float32)
    grads = own_ref[:, :units] + got[:, :units]
    acts = own_ref[:, units:] + (got[:, units : units + 128] + got[:, units + 128 :])
    high = acts.astype(jnp.bfloat16)
    out_ref[:, :units] = grads.astype(jnp.bfloat16)
    out_ref[:, units : units + 128] = high
    out_ref[:, units + 128 :] = (acts - high.astype(jnp.float32)).astype(jnp.bfloat16)


def add_pair(own, got):
    vmem = pl.BlockSpec(memory_space=pltpu.VMEM)
    return pl.pallas_call(
        pair_kernel,
        out_shape=jax.ShapeDtypeStruct(got.shape, jnp.bfloat16),
        in_specs=[vmem, vmem],
        out_specs=vmem,
        compiler_params=pltpu.CompilerParams(vmem_limit_bytes=24 * 1024 * 1024),
        cost_estimate=pl.CostEstimate(
            flops=2 * own.size, bytes_accessed=own.size * 8, transcendentals=0
        ),
    )(own, got)


def score_kernel(acts_at_ref, inv_at_ref, place_ref, grads_ref, own_acts_ref, sib_acts_ref,
                 own_inv_ref, sib_inv_ref, out_ref, train_grads, query_acts, train_acts, inv,
                 sums):
    rows = TQ + TS
    for r in range(GROUPS):
        train_grads[r * TS : (r + 1) * TS, :] = grads_ref[r * rows + TQ : (r + 1) * rows, :]
        for part in range(2):
            start = pl.multiple_of(acts_at_ref[part * GROUPS + r], rows)
            middle = pl.multiple_of(start + TQ, TQ)
            lanes = slice(part * 128, part * 128 + 128)
            for ref, at in ((own_acts_ref, part * 128), (sib_acts_ref, part * 128 + 256)):
                query_acts[r * TQ : (r + 1) * TQ, at : at + 128] = ref[pl.ds(start, TQ), lanes]
                train_acts[r * TS : (r + 1) * TS, at : at + 128] = ref[
                    pl.ds(middle, TS), lanes
                ].astype(jnp.float32)
    same = inv_at_ref[0] == 1
    core_lanes = pl.multiple_of(inv_at_ref[1] * 128, 128)
    other_lanes = pl.multiple_of(128 - inv_at_ref[1] * 128, 128)
    for at, lanes in ((0, core_lanes), (256, other_lanes)):
        mine = own_inv_ref[:, pl.ds(lanes, 128)]
        theirs = sib_inv_ref[:, pl.ds(lanes, 128)]
        inv[:, at : at + 128] = jnp.where(same, mine, theirs)
        inv[:, at + 128 : at + 256] = jnp.where(same, theirs, mine)

    def one_query(n, carry):
        grads = grads_ref[pl.ds(pl.multiple_of(n * rows, rows), TQ), :]
        total = jnp.zeros((GROUPS, 128), jnp.float32)
        for at in (0, 256):
            acts = query_acts[pl.ds(pl.multiple_of(n * TQ, TQ), TQ), at : at + 256]
            gradient = lax.dot_general(
                grads, acts, (((0,), (0,)), ((), ())), preferred_element_type=jnp.float32
            )
            preconditioned = (gradient * inv[:, at : at + 256]).astype(jnp.bfloat16)
            projected = jnp.dot(
                train_grads[...], preconditioned, preferred_element_type=jnp.float32
            )
            terms = projected * train_acts[:, at : at + 256]
            terms = terms.reshape(GROUPS, TS, 256).sum(1)
            total = total + terms[:, :128] + terms[:, 128:]
        sums[pl.ds(n, 1)] = total[None]
        return carry

    lax.fori_loop(0, GROUPS, one_query, 0)
    scores = jnp.sum(sums[...], axis=2)
    hot = place_ref[...]
    scores = jnp.dot(
        hot, jnp.dot(scores, jnp.transpose(hot), precision=lax.Precision.HIGHEST),
        precision=lax.Precision.HIGHEST,
    )
    out_ref[...] = jnp.concatenate(
        [scores, jnp.zeros((GROUPS, 128 - GROUPS), jnp.float32)], 1
    )


def score_blocks(acts_at, inv_at, place, grads, own_acts, sib_acts, own_inv, sib_inv):
    units, features = own_inv.shape
    vmem = pl.BlockSpec(memory_space=pltpu.VMEM)
    smem = pl.BlockSpec(memory_space=pltpu.SMEM)
    return pl.pallas_call(
        score_kernel,
        out_shape=jax.ShapeDtypeStruct((GROUPS, 128), jnp.float32),
        in_specs=[smem] * 2 + [vmem] * 6,
        out_specs=vmem,
        scratch_shapes=[
            pltpu.VMEM((GROUPS * TS, units), jnp.bfloat16),
            pltpu.VMEM((GROUPS * TQ, 2 * features), jnp.bfloat16),
            pltpu.VMEM((GROUPS * TS, 2 * features), jnp.float32),
            pltpu.VMEM((units, 2 * features), jnp.float32),
            pltpu.VMEM((GROUPS, GROUPS, 128), jnp.float32),
        ],
        compiler_params=pltpu.CompilerParams(vmem_limit_bytes=24 * 1024 * 1024),
        cost_estimate=pl.CostEstimate(
            flops=2 * GROUPS * units * 2 * features * (GROUPS * TS + TQ),
            bytes_accessed=8 * 1024 * 1024,
            transcendentals=0,
        ),
    )(acts_at, inv_at, place, grads, own_acts, sib_acts, own_inv, sib_inv)


def shards(query_acts, query_grads, train_acts, train_grads, basis_in, basis_out, eigen):
    in_local = query_acts.shape[2]
    out_local = query_grads.shape[2]
    tokens = jnp.concatenate(
        [
            jnp.concatenate([query_grads[0], query_acts[0]], 1),
            jnp.concatenate([train_grads[0], train_acts[0]], 1),
        ],
        0,
    )
    dp, mp = lax.axis_index("dp"), lax.axis_index("mp")
    z, yl, q, core = dp // NYL, dp % NYL, mp // NC, mp % NC
    units = out_local // 2

    own_inv = 1.0 / (lax.dynamic_slice_in_dim(eigen, core * units, units, 0) + damping)
    sib_eigen = lax.ppermute(
        lax.dynamic_slice_in_dim(eigen, (1 - core) * units, units, 0), "mp", CORE_SWAP
    )
    sib_inv = 1.0 / (sib_eigen + damping)

    turned_basis = lax.ppermute(basis_in, ("dp", "mp"), TRANSPOSE)

    held = ring_gather(tokens)
    kept = []
    for chunk in CHUNKS:
        sib_part, own_part = turn(core, [held[place] for place in chunk], basis_out, turned_basis)
        pair = add_pair(own_part, lax.ppermute(sib_part, "mp", CORE_SWAP))
        parts = exchange(pair, "mp", axis_index_groups=SAME_CORE)
        kept.append(parts.reshape(CHIPS, -1, units + 256).astype(jnp.float32).sum(0))
    kept = jnp.concatenate(kept, 0)

    own_acts = (kept[:, units : units + 128] + kept[:, units + 128 :]).astype(jnp.bfloat16)
    own_acts = lax.ppermute(own_acts, ("dp", "mp"), CHIP_TRANSPOSE)
    own_acts = jnp.concatenate(
        [own_acts, lax.ppermute(own_acts, "dp", dp_shift(0, 1))], 1
    )
    around = z_ring(own_acts)
    own_acts = jnp.concatenate([around[k] for k in RING], 0)
    sib_acts = lax.ppermute(own_acts, "mp", CORE_SWAP)

    all_grads = share(
        kept[:, :units].astype(jnp.bfloat16), CHIPS, "mp", axis_index_groups=SAME_CORE
    )

    dz = jnp.array([CHUNKS[r % 2][r // 2][0] for r in range(GROUPS)], jnp.int32)
    dy = jnp.array([CHUNKS[r % 2][r // 2][1] for r in range(GROUPS)], jnp.int32)
    z_from, y_from = (z + dz + NZ) % NZ, (yl + dy) % NYL
    order = z_from * NYL + y_from
    place = (order[None, :] == jnp.arange(GROUPS, dtype=jnp.int32)[:, None]).astype(jnp.float32)
    at = {place: (half, i) for half in range(2) for i, place in enumerate(CHUNKS[half])}
    places = [(k if k <= 4 else k - NZ, j) for k in range(NZ) for j in range(NYL)]
    half_of = jnp.array([at[place][0] for place in places], jnp.int32)
    chip_of = jnp.array([at[place][1] for place in places], jnp.int32)
    ring_of = jnp.array(
        [RING.index(k if k <= 4 else k - NZ) for k in range(NZ)], jnp.int32
    )

    def stands(row_y):
        where = ((z_from - q + NZ) % NZ) * NYL + (y_from - row_y + NYL) % NYL
        piece = ring_of[(chip_of[where] - z + NZ) % NZ]
        return piece * (2 * (TQ + TS)) + half_of[where] * (TQ + TS)

    acts_at = jnp.concatenate([stands(yl), stands(1 - yl)])
    inv_at = jnp.stack([(yl == core).astype(jnp.int32), core.astype(jnp.int32)])

    scores = score_blocks(
        acts_at, inv_at, place, all_grads, own_acts, sib_acts, own_inv, sib_inv
    )
    normalizer = float(TQ * TS * IN * OUT) ** (-0.5)
    scores = share(scores * normalizer, GROUPS, "mp").reshape(GROUPS, GROUPS, 128).sum(0)
    scores = share(scores, GROUPS, "dp").reshape(GROUPS, GROUPS, 128).sum(0)
    return scores[:, :GROUPS]


def solution(mesh):
    placed = (
        P("dp", None, "mp"),
        P("dp", None, "mp"),
        P("dp", None, "mp"),
        P("dp", None, "mp"),
        P("dp", "mp"),
        P("mp", "dp"),
        P("dp", "mp"),
    )
    return jax.shard_map(shards, mesh=mesh, in_specs=placed, out_specs=P(), check_vma=False)
```

```python
import functools

import jax
import jax.numpy as jnp
from jax import lax
from jax.experimental import pallas as pl
from jax.experimental.pallas import tpu as pltpu
from jax.sharding import PartitionSpec as P

IN = 4096
OUT = 28672
TS = 32
TQ = 32

damping = 0.1

NZ, NYL, NX, NYH, NC = 8, 2, 4, 2, 2
GROUPS = NZ * NYL
CHIPS = NX * NYH


def dp_index(z, yl):
    return (z % NZ) * NYL + yl % NYL


def mp_index(x, yh, core):
    return ((x % NX) * NYH + yh % NYH) * NC + core % NC


def dp_shift(dz, dyl):
    return [
        (dp_index(z, y), dp_index(z + dz, y + dyl)) for z in range(NZ) for y in range(NYL)
    ]


CORE_SWAP = [
    (mp_index(x, h, c), mp_index(x, h, c + 1))
    for x in range(NX)
    for h in range(NYH)
    for c in range(NC)
]
TRANSPOSE = [(d * 16 + m, m * 16 + d) for d in range(16) for m in range(16)]
SAME_CORE = [
    [mp_index(x, h, c) for x in range(NX) for h in range(NYH)] for c in range(NC)
]

CHUNKS = (
    ((0, 0), (0, 1), (1, 0), (-1, 0), (1, 1), (-1, 1), (2, 0), (-2, 0)),
    ((2, 1), (-2, 1), (3, 0), (-3, 0), (3, 1), (-3, 1), (4, 0), (4, 1)),
)


def dp_swap(z_bit, y_bit):
    return [
        (dp_index(z, y), dp_index(z ^ z_bit, y ^ y_bit)) for z in range(NZ) for y in range(NYL)
    ]


DP_SWAPS = tuple(dp_swap(*bits) for bits in ((0, 1), (1, 0), (2, 0), (4, 0)))


def exchange(x, axis, **kw):
    return lax.all_to_all(x, axis, 0, 0, tiled=True, **kw)


def share(x, count, axis, **kw):
    return exchange(jnp.tile(x, (count, 1)), axis, **kw)


def fence_kernel(*refs):
    del refs


def fence(*arrays):
    anywhere = pl.BlockSpec(memory_space=pl.ANY)
    return pl.pallas_call(
        fence_kernel,
        out_shape=[jax.ShapeDtypeStruct(a.shape, a.dtype) for a in arrays],
        in_specs=[anywhere] * len(arrays),
        out_specs=[anywhere] * len(arrays),
        input_output_aliases={i: i for i in range(len(arrays))},
        compiler_params=pltpu.CompilerParams(vmem_limit_bytes=1024 * 1024),
    )(*arrays)


def up(x):
    return lax.ppermute(x, "dp", dp_shift(-1, 0))


def down(x):
    return lax.ppermute(x, "dp", dp_shift(1, 0))


def over(x):
    return lax.ppermute(x, "dp", dp_shift(0, 1))


def turn_kernel(count, core_ref, *refs):
    del core_ref
    blocks, basis_ref = refs[:count], refs[count]
    sib_ref, own_ref, tokens = refs[-3:]
    rows = blocks[0].shape[0]
    step = pl.program_id(0)

    @pl.when(step == 0)
    def _():
        for r, ref in enumerate(blocks):
            tokens[r * rows : (r + 1) * rows, :] = ref[...]
        sib_ref[...] = jnp.dot(
            tokens[...], basis_ref[...], preferred_element_type=jnp.float32
        ).astype(jnp.bfloat16)

    @pl.when(step == 1)
    def _():
        own_ref[...] = jnp.dot(
            tokens[...], basis_ref[...], preferred_element_type=jnp.float32
        )


def turn(core, blocks, basis, needs=()):
    rows, features = blocks[0].shape
    units = basis.shape[1] // 2
    tokens = rows * len(blocks)
    whole = lambda i, core_ref: (0, 0)
    side = lambda i, core_ref: (0, jnp.where(i == 0, 1 - core_ref[0], core_ref[0]))
    return pl.pallas_call(
        functools.partial(turn_kernel, len(blocks)),
        grid_spec=pltpu.PrefetchScalarGridSpec(
            num_scalar_prefetch=1,
            grid=(2,),
            in_specs=[pl.BlockSpec((rows, features), whole)] * len(blocks)
            + [pl.BlockSpec((features, units), side)]
            + [pl.BlockSpec(memory_space=pl.ANY)] * len(needs),
            out_specs=[pl.BlockSpec((tokens, units), whole)] * 2,
            scratch_shapes=[pltpu.VMEM((tokens, features), jnp.bfloat16)],
        ),
        out_shape=[
            jax.ShapeDtypeStruct((tokens, units), jnp.bfloat16),
            jax.ShapeDtypeStruct((tokens, units), jnp.float32),
        ],
        compiler_params=pltpu.CompilerParams(vmem_limit_bytes=56 * 1024 * 1024),
        cost_estimate=pl.CostEstimate(
            flops=2 * tokens * features * units * 2,
            bytes_accessed=2 * tokens * (features + 3 * units) + 4 * features * units,
            transcendentals=0,
        ),
    )(core.reshape(1), *blocks, basis, *needs)


def after(x, y):
    return x + jnp.minimum(jnp.abs(y[:1, :1]), 0).astype(x.dtype)


def sum_kernel(parts_ref, *refs):
    out_ref = refs[-1]
    rows = parts_ref.shape[0] // CHIPS
    total = parts_ref[:rows, :].astype(jnp.float32)
    for i in range(1, CHIPS):
        total = total + parts_ref[i * rows : (i + 1) * rows, :].astype(jnp.float32)
    total = total.astype(jnp.bfloat16)
    for i in range(CHIPS):
        out_ref[i * rows : (i + 1) * rows, :] = total


def sum_and_copy(parts, *needs):
    vmem = pl.BlockSpec(memory_space=pltpu.VMEM)
    return pl.pallas_call(
        sum_kernel,
        out_shape=jax.ShapeDtypeStruct(parts.shape, jnp.bfloat16),
        in_specs=[vmem] + [pl.BlockSpec(memory_space=pl.ANY)] * len(needs),
        out_specs=vmem,
        compiler_params=pltpu.CompilerParams(vmem_limit_bytes=16 * 1024 * 1024),
        cost_estimate=pl.CostEstimate(
            flops=parts.size, bytes_accessed=parts.size * 4, transcendentals=0
        ),
    )(parts, *needs)


def score_kernel(acts_at_ref, place_ref, grads_hbm, own_acts_ref, sib_acts_ref, own_hbm,
                 sib_hbm, out_ref, train_grads, query_acts, train_acts, sums, grads_ref,
                 own_inv_ref, sib_inv_ref, arrived):
    rows = TQ + TS
    copies = [
        pltpu.make_async_copy(source, target, arrived.at[i])
        for i, (source, target) in enumerate(
            ((grads_hbm, grads_ref), (own_hbm, own_inv_ref), (sib_hbm, sib_inv_ref))
        )
    ]
    for copy in copies:
        copy.start()
    for r in range(GROUPS):
        for part, ref in ((0, own_acts_ref), (1, sib_acts_ref)):
            start = pl.multiple_of(acts_at_ref[r], rows)
            middle = pl.multiple_of(start + TQ, TQ)
            lanes = slice(part * 256, part * 256 + 256)
            query_acts[r * TQ : (r + 1) * TQ, lanes] = ref[pl.ds(start, TQ), :]
            train_acts[r * TS : (r + 1) * TS, lanes] = ref[pl.ds(middle, TS), :].astype(
                jnp.float32
            )
    copies[0].wait()
    for r in range(GROUPS):
        train_grads[r * TS : (r + 1) * TS, :] = grads_ref[r * rows + TQ : (r + 1) * rows, :]
    copies[1].wait()
    copies[2].wait()

    def one_query(n):
        grads = grads_ref[pl.ds(pl.multiple_of(n * rows, rows), TQ), :]
        total = jnp.zeros((GROUPS, 128), jnp.float32)
        for at, inv_ref in ((0, own_inv_ref), (256, sib_inv_ref)):
            acts = query_acts[pl.ds(pl.multiple_of(n * TQ, TQ), TQ), at : at + 256]
            gradient = lax.dot_general(
                grads, acts, (((0,), (0,)), ((), ())), preferred_element_type=jnp.float32
            )
            preconditioned = (gradient * inv_ref[...]).astype(jnp.bfloat16)
            projected = jnp.dot(
                train_grads[...], preconditioned, preferred_element_type=jnp.float32
            )
            terms = projected * train_acts[:, at : at + 256]
            terms = terms.reshape(GROUPS, TS, 256).sum(1)
            total = total + terms[:, :128] + terms[:, 128:]
        sums[pl.ds(n, 1)] = total[None]

    def four_queries(i, carry):
        for j in range(4):
            one_query(i * 4 + j)
        return carry

    lax.fori_loop(0, GROUPS // 4, four_queries, 0)
    scores = jnp.sum(sums[...], axis=2)
    hot = place_ref[...]
    scores = jnp.dot(
        hot, jnp.dot(scores, jnp.transpose(hot), precision=lax.Precision.HIGHEST),
        precision=lax.Precision.HIGHEST,
    )
    out_ref[...] = jnp.concatenate(
        [scores, jnp.zeros((GROUPS, 128 - GROUPS), jnp.float32)], 1
    )


def score_blocks(acts_at, place, grads, own_acts, sib_acts, own_inv, sib_inv):
    units, features = own_inv.shape
    vmem = pl.BlockSpec(memory_space=pltpu.VMEM)
    smem = pl.BlockSpec(memory_space=pltpu.SMEM)
    hbm = pl.BlockSpec(memory_space=pl.ANY)
    return pl.pallas_call(
        score_kernel,
        out_shape=jax.ShapeDtypeStruct((GROUPS, 128), jnp.float32),
        in_specs=[smem, vmem, hbm, vmem, vmem, hbm, hbm],
        out_specs=vmem,
        scratch_shapes=[
            pltpu.VMEM((GROUPS * TS, units), jnp.bfloat16),
            pltpu.VMEM((GROUPS * TQ, 2 * features), jnp.bfloat16),
            pltpu.VMEM((GROUPS * TS, 2 * features), jnp.float32),
            pltpu.VMEM((GROUPS, GROUPS, 128), jnp.float32),
            pltpu.VMEM(grads.shape, jnp.bfloat16),
            pltpu.VMEM((units, features), jnp.float32),
            pltpu.VMEM((units, features), jnp.float32),
            pltpu.SemaphoreType.DMA((3,)),
        ],
        compiler_params=pltpu.CompilerParams(vmem_limit_bytes=56 * 1024 * 1024),
        cost_estimate=pl.CostEstimate(
            flops=2 * GROUPS * units * 2 * features * (GROUPS * TS + TQ),
            bytes_accessed=8 * 1024 * 1024,
            transcendentals=0,
        ),
    )(acts_at, place, grads, own_acts, sib_acts, own_inv, sib_inv)


def shards(query_acts, query_grads, train_acts, train_grads, basis_in, basis_out, eigen):
    in_local = query_acts.shape[2]
    out_local = query_grads.shape[2]
    acts = jnp.concatenate([query_acts[0], train_acts[0]], 0)
    grads = jnp.concatenate([query_grads[0], train_grads[0]], 0)
    dp, mp = lax.axis_index("dp"), lax.axis_index("mp")
    z, yl, core = dp // NYL, dp % NYL, mp % NC
    units = out_local // 2
    rows = TQ + TS

    own_inv = 1.0 / (lax.dynamic_slice_in_dim(eigen, core * units, units, 0) + damping)
    sib_eigen = lax.ppermute(
        lax.dynamic_slice_in_dim(eigen, (1 - core) * units, units, 0), "mp", CORE_SWAP
    )
    sib_inv = 1.0 / (sib_eigen + damping)

    held = {(0, 0): grads}
    moved = lax.ppermute(acts, ("dp", "mp"), TRANSPOSE)
    held[(0, 0)], held[(1, 0)], held[(-1, 0)], held[(0, 1)] = fence(
        grads, up(grads), down(grads), over(grads)
    )
    held[(1, 0)], held[(-1, 0)], held[(2, 0)], held[(-2, 0)], held[(1, 1)] = fence(
        held[(1, 0)], held[(-1, 0)], up(held[(1, 0)]), down(held[(-1, 0)]),
        over(held[(1, 0)]),
    )
    (held[(2, 0)], held[(-2, 0)], held[(3, 0)], held[(-3, 0)], held[(1, 1)], held[(-1, 1)],
     moved) = fence(
        held[(2, 0)], held[(-2, 0)], up(held[(2, 0)]), down(held[(-2, 0)]), held[(1, 1)],
        over(held[(-1, 0)]), moved,
    )
    every_acts = share(moved, GROUPS, "mp")
    held[(3, 0)], held[(-3, 0)], held[(2, 1)], held[(-2, 1)], held[(4, 0)], held[(3, 1)] = fence(
        held[(3, 0)], held[(-3, 0)], up(held[(1, 1)]), down(held[(-1, 1)]), down(held[(-3, 0)]),
        over(held[(3, 0)]),
    )
    held[(4, 1)], held[(-3, 1)] = up(held[(3, 1)]), over(held[(-3, 0)])

    summed = jnp.dot(every_acts, basis_in, preferred_element_type=jnp.float32)
    bits = (yl, z % 2, z // 2 % 2, z // 4)
    sums = []
    for k, (swap, bit) in enumerate(zip(DP_SWAPS, bits)):
        half = summed.shape[0] // 2
        away = lax.dynamic_slice_in_dim(summed, (1 - bit) * half, half, 0)
        mine = lax.dynamic_slice_in_dim(summed, bit * half, half, 0)
        if k == 0:
            first = away = away.astype(jnp.bfloat16)
        summed = mine + lax.ppermute(away, "dp", swap).astype(jnp.float32)
        sums.append(summed)
    own_acts = summed.astype(jnp.bfloat16)

    pairs = []
    for chunk, needs in zip(CHUNKS, ((held[(3, 1)],), (own_inv, sib_inv, first))):
        sib_part, own_part = turn(core, [held[place] for place in chunk], basis_out, needs)
        got = lax.ppermute(sib_part, "mp", CORE_SWAP).astype(jnp.float32)
        if pairs:
            got = after(got, sums[0])
        pairs.append((own_part + got).astype(jnp.bfloat16))
    pairs = jnp.concatenate(pairs, 0)
    parts = exchange(pairs, "mp", axis_index_groups=SAME_CORE)
    copies = sum_and_copy(parts)

    own_acts = after(own_acts, copies)
    for swap in DP_SWAPS[::-1]:
        own_acts = jnp.concatenate([own_acts, lax.ppermute(own_acts, "dp", swap)], 0)
    sib_acts = lax.ppermute(own_acts, "mp", CORE_SWAP)

    all_grads = exchange(copies, "mp", axis_index_groups=SAME_CORE)

    places = [place for chunk in CHUNKS for place in chunk]
    dz = jnp.array([p[0] for p in places], jnp.int32)
    dy = jnp.array([p[1] for p in places], jnp.int32)
    order = ((z + dz + NZ) % NZ) * NYL + (yl + dy) % NYL
    place = (order[None, :] == jnp.arange(GROUPS, dtype=jnp.int32)[:, None]).astype(jnp.float32)

    kept = bits[0] * 8 + bits[1] * 4 + bits[2] * 2 + bits[3]
    acts_at = (order ^ kept) * rows

    scores = score_blocks(
        acts_at, place, all_grads, own_acts, sib_acts, own_inv, sib_inv
    )
    normalizer = float(TQ * TS * IN * OUT) ** (-0.5)
    scores = share(scores * normalizer, GROUPS, "mp").reshape(GROUPS, GROUPS, 128).sum(0)
    scores = share(scores, GROUPS, "dp").reshape(GROUPS, GROUPS, 128).sum(0)
    return scores[:, :GROUPS]


def solution(mesh):
    placed = (
        P("dp", None, "mp"),
        P("dp", None, "mp"),
        P("dp", None, "mp"),
        P("dp", None, "mp"),
        P("dp", "mp"),
        P("mp", "dp"),
        P("dp", "mp"),
    )
    return jax.shard_map(shards, mesh=mesh, in_specs=placed, out_specs=P(), check_vma=False)
```

```python
import functools

import jax
import jax.numpy as jnp
from jax import lax
from jax.experimental import pallas as pl
from jax.experimental.pallas import tpu as pltpu
from jax.sharding import PartitionSpec as P

IN = 4096
OUT = 28672
TS = 32
TQ = 32

damping = 0.1

NZ, NYL, NX, NYH, NC = 8, 2, 4, 2, 2
GROUPS = NZ * NYL
CHIPS = NX * NYH


def dp_index(z, yl):
    return (z % NZ) * NYL + yl % NYL


def mp_index(x, yh, core):
    return ((x % NX) * NYH + yh % NYH) * NC + core % NC


def dp_shift(dz, dyl):
    return [
        (dp_index(z, y), dp_index(z + dz, y + dyl)) for z in range(NZ) for y in range(NYL)
    ]


CORE_SWAP = [
    (mp_index(x, h, c), mp_index(x, h, c + 1))
    for x in range(NX)
    for h in range(NYH)
    for c in range(NC)
]
TRANSPOSE = [(d * 16 + m, m * 16 + d) for d in range(16) for m in range(16)]
SAME_CORE = [
    [mp_index(x, h, c) for x in range(NX) for h in range(NYH)] for c in range(NC)
]

CHUNKS = (
    ((0, 0), (0, 1), (1, 0), (-1, 0), (1, 1), (-1, 1), (2, 0), (-2, 0)),
    ((2, 1), (-2, 1), (3, 0), (-3, 0), (3, 1), (-3, 1), (4, 0), (4, 1)),
)


def dp_swap(z_bit, y_bit):
    return [
        (dp_index(z, y), dp_index(z ^ z_bit, y ^ y_bit)) for z in range(NZ) for y in range(NYL)
    ]


DP_SWAPS = tuple(dp_swap(*bits) for bits in ((0, 1), (1, 0), (2, 0), (4, 0)))


def exchange(x, axis, **kw):
    return lax.all_to_all(x, axis, 0, 0, tiled=True, **kw)


def share(x, count, axis, **kw):
    return exchange(jnp.tile(x, (count, 1)), axis, **kw)


def fence_kernel(*refs):
    del refs


def fence(*arrays):
    anywhere = pl.BlockSpec(memory_space=pl.ANY)
    return pl.pallas_call(
        fence_kernel,
        out_shape=[jax.ShapeDtypeStruct(a.shape, a.dtype) for a in arrays],
        in_specs=[anywhere] * len(arrays),
        out_specs=[anywhere] * len(arrays),
        input_output_aliases={i: i for i in range(len(arrays))},
        compiler_params=pltpu.CompilerParams(vmem_limit_bytes=1024 * 1024),
    )(*arrays)


def up(x):
    return lax.ppermute(x, "dp", dp_shift(-1, 0))


def down(x):
    return lax.ppermute(x, "dp", dp_shift(1, 0))


def over(x):
    return lax.ppermute(x, "dp", dp_shift(0, 1))


def turn_kernel(count, core_ref, *refs):
    del core_ref
    blocks, basis_ref = refs[:count], refs[count]
    sib_ref, own_ref, tokens = refs[-3:]
    rows = blocks[0].shape[0]
    step = pl.program_id(0)

    @pl.when(step == 0)
    def _():
        for r, ref in enumerate(blocks):
            tokens[r * rows : (r + 1) * rows, :] = ref[...]
        sib_ref[...] = jnp.dot(
            tokens[...], basis_ref[...], preferred_element_type=jnp.float32
        ).astype(jnp.bfloat16)

    @pl.when(step == 1)
    def _():
        own_ref[...] = jnp.dot(
            tokens[...], basis_ref[...], preferred_element_type=jnp.float32
        )


def turn(core, blocks, basis, needs=()):
    rows, features = blocks[0].shape
    units = basis.shape[1] // 2
    tokens = rows * len(blocks)
    whole = lambda i, core_ref: (0, 0)
    side = lambda i, core_ref: (0, jnp.where(i == 0, 1 - core_ref[0], core_ref[0]))
    return pl.pallas_call(
        functools.partial(turn_kernel, len(blocks)),
        grid_spec=pltpu.PrefetchScalarGridSpec(
            num_scalar_prefetch=1,
            grid=(2,),
            in_specs=[pl.BlockSpec((rows, features), whole)] * len(blocks)
            + [pl.BlockSpec((features, units), side)]
            + [pl.BlockSpec(memory_space=pl.ANY)] * len(needs),
            out_specs=[pl.BlockSpec((tokens, units), whole)] * 2,
            scratch_shapes=[pltpu.VMEM((tokens, features), jnp.bfloat16)],
        ),
        out_shape=[
            jax.ShapeDtypeStruct((tokens, units), jnp.bfloat16),
            jax.ShapeDtypeStruct((tokens, units), jnp.float32),
        ],
        compiler_params=pltpu.CompilerParams(vmem_limit_bytes=56 * 1024 * 1024),
        cost_estimate=pl.CostEstimate(
            flops=2 * tokens * features * units * 2,
            bytes_accessed=2 * tokens * (features + 3 * units) + 4 * features * units,
            transcendentals=0,
        ),
    )(core.reshape(1), *blocks, basis, *needs)


def sum_kernel(parts_ref, *refs):
    out_ref = refs[-1]
    rows = parts_ref.shape[0] // CHIPS
    total = parts_ref[:rows, :].astype(jnp.float32)
    for i in range(1, CHIPS):
        total = total + parts_ref[i * rows : (i + 1) * rows, :].astype(jnp.float32)
    total = total.astype(jnp.bfloat16)
    for i in range(CHIPS):
        out_ref[i * rows : (i + 1) * rows, :] = total


def sum_and_copy(parts, *needs):
    vmem = pl.BlockSpec(memory_space=pltpu.VMEM)
    return pl.pallas_call(
        sum_kernel,
        out_shape=jax.ShapeDtypeStruct(parts.shape, jnp.bfloat16),
        in_specs=[vmem] + [pl.BlockSpec(memory_space=pl.ANY)] * len(needs),
        out_specs=vmem,
        compiler_params=pltpu.CompilerParams(vmem_limit_bytes=16 * 1024 * 1024),
        cost_estimate=pl.CostEstimate(
            flops=parts.size, bytes_accessed=parts.size * 4, transcendentals=0
        ),
    )(parts, *needs)


def score_kernel(acts_at_ref, place_ref, grads_hbm, own_acts_ref, sib_acts_ref, own_hbm,
                 sib_hbm, out_ref, train_grads, query_acts, train_acts, sums, grads_ref,
                 own_inv_ref, sib_inv_ref, arrived):
    rows = TQ + TS
    copies = [
        pltpu.make_async_copy(source, target, arrived.at[i])
        for i, (source, target) in enumerate(
            ((grads_hbm, grads_ref), (own_hbm, own_inv_ref), (sib_hbm, sib_inv_ref))
        )
    ]
    for copy in copies:
        copy.start()
    for r in range(GROUPS):
        for part, ref in ((0, own_acts_ref), (1, sib_acts_ref)):
            start = pl.multiple_of(acts_at_ref[r], rows)
            middle = pl.multiple_of(start + TQ, TQ)
            lanes = slice(part * 256, part * 256 + 256)
            query_acts[r * TQ : (r + 1) * TQ, lanes] = ref[pl.ds(start, TQ), :]
            train_acts[r * TS : (r + 1) * TS, lanes] = ref[pl.ds(middle, TS), :].astype(
                jnp.float32
            )
    copies[0].wait()
    for r in range(GROUPS):
        train_grads[r * TS : (r + 1) * TS, :] = grads_ref[r * rows + TQ : (r + 1) * rows, :]
    copies[1].wait()
    copies[2].wait()

    def one_query(n):
        grads = grads_ref[pl.ds(pl.multiple_of(n * rows, rows), TQ), :]
        total = jnp.zeros((GROUPS, 128), jnp.float32)
        for at, inv_ref in ((0, own_inv_ref), (256, sib_inv_ref)):
            acts = query_acts[pl.ds(pl.multiple_of(n * TQ, TQ), TQ), at : at + 256]
            gradient = lax.dot_general(
                grads, acts, (((0,), (0,)), ((), ())), preferred_element_type=jnp.float32
            )
            preconditioned = (gradient * inv_ref[...]).astype(jnp.bfloat16)
            projected = jnp.dot(
                train_grads[...], preconditioned, preferred_element_type=jnp.float32
            )
            terms = projected * train_acts[:, at : at + 256]
            terms = terms.reshape(GROUPS, TS, 256).sum(1)
            total = total + terms[:, :128] + terms[:, 128:]
        sums[pl.ds(n, 1)] = total[None]

    def four_queries(i, carry):
        for j in range(4):
            one_query(i * 4 + j)
        return carry

    lax.fori_loop(0, GROUPS // 4, four_queries, 0)
    scores = jnp.sum(sums[...], axis=2)
    hot = place_ref[...]
    scores = jnp.dot(
        hot, jnp.dot(scores, jnp.transpose(hot), precision=lax.Precision.HIGHEST),
        precision=lax.Precision.HIGHEST,
    )
    out_ref[...] = jnp.concatenate(
        [scores, jnp.zeros((GROUPS, 128 - GROUPS), jnp.float32)], 1
    )


def score_blocks(acts_at, place, grads, own_acts, sib_acts, own_inv, sib_inv):
    units, features = own_inv.shape
    vmem = pl.BlockSpec(memory_space=pltpu.VMEM)
    smem = pl.BlockSpec(memory_space=pltpu.SMEM)
    hbm = pl.BlockSpec(memory_space=pl.ANY)
    return pl.pallas_call(
        score_kernel,
        out_shape=jax.ShapeDtypeStruct((GROUPS, 128), jnp.float32),
        in_specs=[smem, vmem, hbm, vmem, vmem, hbm, hbm],
        out_specs=vmem,
        scratch_shapes=[
            pltpu.VMEM((GROUPS * TS, units), jnp.bfloat16),
            pltpu.VMEM((GROUPS * TQ, 2 * features), jnp.bfloat16),
            pltpu.VMEM((GROUPS * TS, 2 * features), jnp.float32),
            pltpu.VMEM((GROUPS, GROUPS, 128), jnp.float32),
            pltpu.VMEM(grads.shape, jnp.bfloat16),
            pltpu.VMEM((units, features), jnp.float32),
            pltpu.VMEM((units, features), jnp.float32),
            pltpu.SemaphoreType.DMA((3,)),
        ],
        compiler_params=pltpu.CompilerParams(vmem_limit_bytes=56 * 1024 * 1024),
        cost_estimate=pl.CostEstimate(
            flops=2 * GROUPS * units * 2 * features * (GROUPS * TS + TQ),
            bytes_accessed=8 * 1024 * 1024,
            transcendentals=0,
        ),
    )(acts_at, place, grads, own_acts, sib_acts, own_inv, sib_inv)


def shards(query_acts, query_grads, train_acts, train_grads, basis_in, basis_out, eigen):
    in_local = query_acts.shape[2]
    out_local = query_grads.shape[2]
    acts = jnp.concatenate([query_acts[0], train_acts[0]], 0)
    grads = jnp.concatenate([query_grads[0], train_grads[0]], 0)
    dp, mp = lax.axis_index("dp"), lax.axis_index("mp")
    z, yl, core = dp // NYL, dp % NYL, mp % NC
    units = out_local // 2
    rows = TQ + TS

    own_inv = 1.0 / (lax.dynamic_slice_in_dim(eigen, core * units, units, 0) + damping)
    sib_eigen = lax.ppermute(
        lax.dynamic_slice_in_dim(eigen, (1 - core) * units, units, 0), "mp", CORE_SWAP
    )
    sib_inv = 1.0 / (sib_eigen + damping)

    held = {(0, 0): grads}
    moved = lax.ppermute(acts, ("dp", "mp"), TRANSPOSE)
    held[(0, 0)], held[(1, 0)], held[(-1, 0)], held[(0, 1)] = fence(
        grads, up(grads), down(grads), over(grads)
    )
    (held[(1, 0)], held[(-1, 0)], held[(2, 0)], held[(-2, 0)], held[(1, 1)], moved, own_inv,
     sib_inv) = fence(
        held[(1, 0)], held[(-1, 0)], up(held[(1, 0)]), down(held[(-1, 0)]),
        over(held[(1, 0)]), moved, own_inv, sib_inv,
    )
    (held[(2, 0)], held[(-2, 0)], held[(3, 0)], held[(-3, 0)], held[(1, 1)], held[(-1, 1)],
     every_acts) = fence(
        held[(2, 0)], held[(-2, 0)], up(held[(2, 0)]), down(held[(-2, 0)]), held[(1, 1)],
        over(held[(-1, 0)]), share(moved, GROUPS, "mp"),
    )

    bits = (yl, z % 2, z // 2 % 2, z // 4)

    def halves(x, bit):
        half = x.shape[0] // 2
        return (
            lax.dynamic_slice_in_dim(x, bit * half, half, 0),
            lax.dynamic_slice_in_dim(x, (1 - bit) * half, half, 0),
        )

    mine, away = halves(
        jnp.dot(every_acts, basis_in, preferred_element_type=jnp.float32), bits[0]
    )
    (held[(3, 0)], held[(-3, 0)], held[(2, 1)], held[(-2, 1)], held[(4, 0)], held[(3, 1)],
     away) = fence(
        held[(3, 0)], held[(-3, 0)], up(held[(1, 1)]), down(held[(-1, 1)]), down(held[(-3, 0)]),
        over(held[(3, 0)]), away.astype(jnp.bfloat16),
    )
    held[(4, 1)], held[(-3, 1)] = up(held[(3, 1)]), over(held[(-3, 0)])
    first = mine + lax.ppermute(away, "dp", DP_SWAPS[0]).astype(jnp.float32)
    summed = first
    for swap, bit in zip(DP_SWAPS[1:], bits[1:]):
        mine, away = halves(summed, bit)
        summed = mine + lax.ppermute(away, "dp", swap)
    own_acts = summed.astype(jnp.bfloat16)

    pairs = []
    for chunk, needs in zip(CHUNKS, ((held[(3, 1)],), (first,))):
        sib_part, own_part = turn(core, [held[place] for place in chunk], basis_out, needs)
        got = lax.ppermute(sib_part, "mp", CORE_SWAP)
        pairs.append((own_part + got.astype(jnp.float32)).astype(jnp.bfloat16))
    parts = exchange(jnp.concatenate(pairs, 0), "mp", axis_index_groups=SAME_CORE)

    doubled = []
    for swap in DP_SWAPS[::-1]:
        own_acts = jnp.concatenate([own_acts, lax.ppermute(own_acts, "dp", swap)], 0)
        doubled.append(own_acts)
    sib_acts = lax.ppermute(own_acts, "mp", CORE_SWAP)

    copies = sum_and_copy(parts, doubled[0])
    all_grads = exchange(copies, "mp", axis_index_groups=SAME_CORE)

    places = [place for chunk in CHUNKS for place in chunk]
    dz = jnp.array([p[0] for p in places], jnp.int32)
    dy = jnp.array([p[1] for p in places], jnp.int32)
    order = ((z + dz + NZ) % NZ) * NYL + (yl + dy) % NYL
    place = (order[None, :] == jnp.arange(GROUPS, dtype=jnp.int32)[:, None]).astype(jnp.float32)

    kept = bits[0] * 8 + bits[1] * 4 + bits[2] * 2 + bits[3]
    acts_at = (order ^ kept) * rows

    scores = score_blocks(
        acts_at, place, all_grads, own_acts, sib_acts, own_inv, sib_inv
    )
    normalizer = float(TQ * TS * IN * OUT) ** (-0.5)
    scores = share(scores * normalizer, GROUPS, "mp").reshape(GROUPS, GROUPS, 128).sum(0)
    scores = share(scores, GROUPS, "dp").reshape(GROUPS, GROUPS, 128).sum(0)
    return scores[:, :GROUPS]


def solution(mesh):
    placed = (
        P("dp", None, "mp"),
        P("dp", None, "mp"),
        P("dp", None, "mp"),
        P("dp", None, "mp"),
        P("dp", "mp"),
        P("mp", "dp"),
        P("dp", "mp"),
    )
    return jax.shard_map(shards, mesh=mesh, in_specs=placed, out_specs=P(), check_vma=False)
```

```python
import functools

import jax
import jax.numpy as jnp
from jax import lax
from jax.experimental import pallas as pl
from jax.experimental.pallas import tpu as pltpu
from jax.sharding import PartitionSpec as P

IN = 4096
OUT = 28672
TS = 32
TQ = 32

damping = 0.1

NZ, NYL, NX, NYH, NC = 8, 2, 4, 2, 2
GROUPS = NZ * NYL
CHIPS = NX * NYH


def dp_index(z, yl):
    return (z % NZ) * NYL + yl % NYL


def mp_index(x, yh, core):
    return ((x % NX) * NYH + yh % NYH) * NC + core % NC


def dp_shift(dz, dyl):
    return [
        (dp_index(z, y), dp_index(z + dz, y + dyl)) for z in range(NZ) for y in range(NYL)
    ]


CORE_SWAP = [
    (mp_index(x, h, c), mp_index(x, h, c + 1))
    for x in range(NX)
    for h in range(NYH)
    for c in range(NC)
]
TRANSPOSE = [(d * 16 + m, m * 16 + d) for d in range(16) for m in range(16)]
SAME_CORE = [
    [mp_index(x, h, c) for x in range(NX) for h in range(NYH)] for c in range(NC)
]

CHUNKS = (
    ((0, 0), (0, 1), (1, 0), (-1, 0), (1, 1), (-1, 1), (2, 0), (-2, 0)),
    ((2, 1), (-2, 1), (3, 0), (-3, 0), (3, 1), (-3, 1), (4, 0), (4, 1)),
)


def dp_swap(z_bit, y_bit):
    return [
        (dp_index(z, y), dp_index(z ^ z_bit, y ^ y_bit)) for z in range(NZ) for y in range(NYL)
    ]


DP_SWAPS = tuple(dp_swap(*bits) for bits in ((0, 1), (1, 0), (2, 0), (4, 0)))


def exchange(x, axis, **kw):
    return lax.all_to_all(x, axis, 0, 0, tiled=True, **kw)


def share(x, count, axis, **kw):
    return exchange(jnp.tile(x, (count, 1)), axis, **kw)


def fence_kernel(*refs):
    del refs


def fence(*arrays, needs=()):
    anywhere = pl.BlockSpec(memory_space=pl.ANY)
    return pl.pallas_call(
        fence_kernel,
        out_shape=[jax.ShapeDtypeStruct(a.shape, a.dtype) for a in arrays],
        in_specs=[anywhere] * (len(arrays) + len(needs)),
        out_specs=[anywhere] * len(arrays),
        input_output_aliases={i: i for i in range(len(arrays))},
        compiler_params=pltpu.CompilerParams(vmem_limit_bytes=1024 * 1024),
    )(*arrays, *needs)


def up(x):
    return lax.ppermute(x, "dp", dp_shift(-1, 0))


def down(x):
    return lax.ppermute(x, "dp", dp_shift(1, 0))


def over(x):
    return lax.ppermute(x, "dp", dp_shift(0, 1))


def turn_kernel(count, core_ref, *refs):
    del core_ref
    blocks, basis_ref = refs[:count], refs[count]
    sib_ref, own_ref, tokens = refs[-3:]
    rows = blocks[0].shape[0]
    step = pl.program_id(0)

    @pl.when(step == 0)
    def _():
        for r, ref in enumerate(blocks):
            tokens[r * rows : (r + 1) * rows, :] = ref[...]
        sib_ref[...] = jnp.dot(
            tokens[...], basis_ref[...], preferred_element_type=jnp.float32
        ).astype(jnp.bfloat16)

    @pl.when(step == 1)
    def _():
        own_ref[...] = jnp.dot(
            tokens[...], basis_ref[...], preferred_element_type=jnp.float32
        )


def turn(core, blocks, basis, needs=()):
    rows, features = blocks[0].shape
    units = basis.shape[1] // 2
    tokens = rows * len(blocks)
    whole = lambda i, core_ref: (0, 0)
    side = lambda i, core_ref: (0, jnp.where(i == 0, 1 - core_ref[0], core_ref[0]))
    return pl.pallas_call(
        functools.partial(turn_kernel, len(blocks)),
        grid_spec=pltpu.PrefetchScalarGridSpec(
            num_scalar_prefetch=1,
            grid=(2,),
            in_specs=[pl.BlockSpec((rows, features), whole)] * len(blocks)
            + [pl.BlockSpec((features, units), side)]
            + [pl.BlockSpec(memory_space=pl.ANY)] * len(needs),
            out_specs=[pl.BlockSpec((tokens, units), whole)] * 2,
            scratch_shapes=[pltpu.VMEM((tokens, features), jnp.bfloat16)],
        ),
        out_shape=[
            jax.ShapeDtypeStruct((tokens, units), jnp.bfloat16),
            jax.ShapeDtypeStruct((tokens, units), jnp.float32),
        ],
        compiler_params=pltpu.CompilerParams(vmem_limit_bytes=56 * 1024 * 1024),
        cost_estimate=pl.CostEstimate(
            flops=2 * tokens * features * units * 2,
            bytes_accessed=2 * tokens * (features + 3 * units) + 4 * features * units,
            transcendentals=0,
        ),
    )(core.reshape(1), *blocks, basis, *needs)


def after(x, y):
    return x + jnp.minimum(jnp.abs(y[:1, :1]), 0).astype(x.dtype)


def sum_kernel(parts_ref, *refs):
    out_ref = refs[-1]
    rows = parts_ref.shape[0] // CHIPS
    total = parts_ref[:rows, :].astype(jnp.float32)
    for i in range(1, CHIPS):
        total = total + parts_ref[i * rows : (i + 1) * rows, :].astype(jnp.float32)
    total = total.astype(jnp.bfloat16)
    for i in range(CHIPS):
        out_ref[i * rows : (i + 1) * rows, :] = total


def sum_and_copy(parts, *needs):
    vmem = pl.BlockSpec(memory_space=pltpu.VMEM)
    return pl.pallas_call(
        sum_kernel,
        out_shape=jax.ShapeDtypeStruct(parts.shape, jnp.bfloat16),
        in_specs=[vmem] + [pl.BlockSpec(memory_space=pl.ANY)] * len(needs),
        out_specs=vmem,
        compiler_params=pltpu.CompilerParams(vmem_limit_bytes=16 * 1024 * 1024),
        cost_estimate=pl.CostEstimate(
            flops=parts.size, bytes_accessed=parts.size * 4, transcendentals=0
        ),
    )(parts, *needs)


def score_kernel(acts_at_ref, place_ref, grads_hbm, own_acts_ref, sib_acts_ref, own_hbm,
                 sib_hbm, out_ref, train_grads, query_acts, train_acts, sums, grads_ref,
                 own_inv_ref, sib_inv_ref, arrived):
    rows = TQ + TS
    copies = [
        pltpu.make_async_copy(source, target, arrived.at[i])
        for i, (source, target) in enumerate(
            ((grads_hbm, grads_ref), (own_hbm, own_inv_ref), (sib_hbm, sib_inv_ref))
        )
    ]
    for copy in copies:
        copy.start()
    for r in range(GROUPS):
        for part, ref in ((0, own_acts_ref), (1, sib_acts_ref)):
            start = pl.multiple_of(acts_at_ref[r], rows)
            middle = pl.multiple_of(start + TQ, TQ)
            lanes = slice(part * 256, part * 256 + 256)
            query_acts[r * TQ : (r + 1) * TQ, lanes] = ref[pl.ds(start, TQ), :]
            train_acts[r * TS : (r + 1) * TS, lanes] = ref[pl.ds(middle, TS), :].astype(
                jnp.float32
            )
    copies[0].wait()
    for r in range(GROUPS):
        train_grads[r * TS : (r + 1) * TS, :] = grads_ref[r * rows + TQ : (r + 1) * rows, :]
    copies[1].wait()
    copies[2].wait()

    def one_query(n):
        grads = grads_ref[pl.ds(pl.multiple_of(n * rows, rows), TQ), :]
        total = jnp.zeros((GROUPS, 128), jnp.float32)
        for at, inv_ref in ((0, own_inv_ref), (256, sib_inv_ref)):
            acts = query_acts[pl.ds(pl.multiple_of(n * TQ, TQ), TQ), at : at + 256]
            gradient = lax.dot_general(
                grads, acts, (((0,), (0,)), ((), ())), preferred_element_type=jnp.float32
            )
            preconditioned = (gradient * inv_ref[...]).astype(jnp.bfloat16)
            projected = jnp.dot(
                train_grads[...], preconditioned, preferred_element_type=jnp.float32
            )
            terms = projected * train_acts[:, at : at + 256]
            terms = terms.reshape(GROUPS, TS, 256).sum(1)
            total = total + terms[:, :128] + terms[:, 128:]
        sums[pl.ds(n, 1)] = total[None]

    def four_queries(i, carry):
        for j in range(4):
            one_query(i * 4 + j)
        return carry

    lax.fori_loop(0, GROUPS // 4, four_queries, 0)
    scores = jnp.sum(sums[...], axis=2)
    hot = place_ref[...]
    scores = jnp.dot(
        hot, jnp.dot(scores, jnp.transpose(hot), precision=lax.Precision.HIGHEST),
        precision=lax.Precision.HIGHEST,
    )
    out_ref[...] = jnp.concatenate(
        [scores, jnp.zeros((GROUPS, 128 - GROUPS), jnp.float32)], 1
    )


def score_blocks(acts_at, place, grads, own_acts, sib_acts, own_inv, sib_inv):
    units, features = own_inv.shape
    vmem = pl.BlockSpec(memory_space=pltpu.VMEM)
    smem = pl.BlockSpec(memory_space=pltpu.SMEM)
    hbm = pl.BlockSpec(memory_space=pl.ANY)
    return pl.pallas_call(
        score_kernel,
        out_shape=jax.ShapeDtypeStruct((GROUPS, 128), jnp.float32),
        in_specs=[smem, vmem, hbm, vmem, vmem, hbm, hbm],
        out_specs=vmem,
        scratch_shapes=[
            pltpu.VMEM((GROUPS * TS, units), jnp.bfloat16),
            pltpu.VMEM((GROUPS * TQ, 2 * features), jnp.bfloat16),
            pltpu.VMEM((GROUPS * TS, 2 * features), jnp.float32),
            pltpu.VMEM((GROUPS, GROUPS, 128), jnp.float32),
            pltpu.VMEM(grads.shape, jnp.bfloat16),
            pltpu.VMEM((units, features), jnp.float32),
            pltpu.VMEM((units, features), jnp.float32),
            pltpu.SemaphoreType.DMA((3,)),
        ],
        compiler_params=pltpu.CompilerParams(vmem_limit_bytes=56 * 1024 * 1024),
        cost_estimate=pl.CostEstimate(
            flops=2 * GROUPS * units * 2 * features * (GROUPS * TS + TQ),
            bytes_accessed=8 * 1024 * 1024,
            transcendentals=0,
        ),
    )(acts_at, place, grads, own_acts, sib_acts, own_inv, sib_inv)


def shards(query_acts, query_grads, train_acts, train_grads, basis_in, basis_out, eigen):
    in_local = query_acts.shape[2]
    out_local = query_grads.shape[2]
    acts = jnp.concatenate([query_acts[0], train_acts[0]], 0)
    grads = jnp.concatenate([query_grads[0], train_grads[0]], 0)
    dp, mp = lax.axis_index("dp"), lax.axis_index("mp")
    z, yl, core = dp // NYL, dp % NYL, mp % NC
    units = out_local // 2
    rows = TQ + TS

    own_inv = 1.0 / (lax.dynamic_slice_in_dim(eigen, core * units, units, 0) + damping)
    sib_eigen = lax.ppermute(
        lax.dynamic_slice_in_dim(eigen, (1 - core) * units, units, 0), "mp", CORE_SWAP
    )
    sib_inv = 1.0 / (sib_eigen + damping)

    held = {(0, 0): grads}
    moved = lax.ppermute(acts, ("dp", "mp"), TRANSPOSE)
    held[(0, 0)], held[(1, 0)], held[(-1, 0)], held[(0, 1)] = fence(
        grads, up(grads), down(grads), over(grads)
    )
    held[(1, 0)], held[(-1, 0)], held[(2, 0)], held[(-2, 0)], held[(1, 1)], moved = fence(
        held[(1, 0)], held[(-1, 0)], up(held[(1, 0)]), down(held[(-1, 0)]),
        over(held[(1, 0)]), moved, needs=(own_inv, sib_inv),
    )
    every_acts = share(moved, GROUPS, "mp")
    held[(2, 0)], held[(-2, 0)], held[(3, 0)], held[(-3, 0)], held[(1, 1)], held[(-1, 1)] = fence(
        held[(2, 0)], held[(-2, 0)], up(held[(2, 0)]), down(held[(-2, 0)]), held[(1, 1)],
        over(held[(-1, 0)]),
    )

    bits = (yl, z % 2, z // 2 % 2, z // 4)

    def halves(x, bit):
        half = x.shape[0] // 2
        return (
            lax.dynamic_slice_in_dim(x, bit * half, half, 0),
            lax.dynamic_slice_in_dim(x, (1 - bit) * half, half, 0),
        )

    mine, away = halves(
        jnp.dot(every_acts, basis_in, preferred_element_type=jnp.float32), bits[0]
    )
    (held[(3, 0)], held[(-3, 0)], held[(2, 1)], held[(-2, 1)], held[(4, 0)], held[(3, 1)],
     away) = fence(
        held[(3, 0)], held[(-3, 0)], up(held[(1, 1)]), down(held[(-1, 1)]), down(held[(-3, 0)]),
        over(held[(3, 0)]), away.astype(jnp.bfloat16),
    )
    held[(4, 1)], held[(-3, 1)] = up(held[(3, 1)]), over(held[(-3, 0)])
    first = mine + lax.ppermute(away, "dp", DP_SWAPS[0]).astype(jnp.float32)
    summed = first
    for swap, bit in zip(DP_SWAPS[1:], bits[1:]):
        mine, away = halves(summed, bit)
        summed = mine + lax.ppermute(away, "dp", swap)
    own_acts = summed.astype(jnp.bfloat16)

    pairs = []
    for chunk, needs in zip(CHUNKS, ((held[(3, 1)],), (first,))):
        sib_part, own_part = turn(core, [held[place] for place in chunk], basis_out, needs)
        got = lax.ppermute(sib_part, "mp", CORE_SWAP)
        pairs.append((own_part + got.astype(jnp.float32)).astype(jnp.bfloat16))
    parts = exchange(jnp.concatenate(pairs, 0), "mp", axis_index_groups=SAME_CORE)

    copies = sum_and_copy(parts)

    own_acts = after(own_acts, copies)
    for swap in DP_SWAPS[::-1]:
        own_acts = jnp.concatenate([own_acts, lax.ppermute(own_acts, "dp", swap)], 0)
    sib_acts = lax.ppermute(own_acts, "mp", CORE_SWAP)

    all_grads = exchange(copies, "mp", axis_index_groups=SAME_CORE)

    places = [place for chunk in CHUNKS for place in chunk]
    dz = jnp.array([p[0] for p in places], jnp.int32)
    dy = jnp.array([p[1] for p in places], jnp.int32)
    order = ((z + dz + NZ) % NZ) * NYL + (yl + dy) % NYL
    place = (order[None, :] == jnp.arange(GROUPS, dtype=jnp.int32)[:, None]).astype(jnp.float32)

    kept = bits[0] * 8 + bits[1] * 4 + bits[2] * 2 + bits[3]
    acts_at = (order ^ kept) * rows

    scores = score_blocks(
        acts_at, place, all_grads, own_acts, sib_acts, own_inv, sib_inv
    )
    normalizer = float(TQ * TS * IN * OUT) ** (-0.5)
    scores = share(scores * normalizer, GROUPS, "mp").reshape(GROUPS, GROUPS, 128).sum(0)
    scores = share(scores, GROUPS, "dp").reshape(GROUPS, GROUPS, 128).sum(0)
    return scores[:, :GROUPS]


def solution(mesh):
    placed = (
        P("dp", None, "mp"),
        P("dp", None, "mp"),
        P("dp", None, "mp"),
        P("dp", None, "mp"),
        P("dp", "mp"),
        P("mp", "dp"),
        P("dp", "mp"),
    )
    return jax.shard_map(shards, mesh=mesh, in_specs=placed, out_specs=P(), check_vma=False)
```

```python
import functools

import jax
import jax.numpy as jnp
from jax import lax
from jax.experimental import pallas as pl
from jax.experimental.pallas import tpu as pltpu
from jax.sharding import PartitionSpec as P

IN = 4096
OUT = 28672
TS = 32
TQ = 32

damping = 0.1

NZ, NYL, NX, NYH, NC = 8, 2, 4, 2, 2
GROUPS = NZ * NYL
CHIPS = NX * NYH


def dp_index(z, yl):
    return (z % NZ) * NYL + yl % NYL


def mp_index(x, yh, core):
    return ((x % NX) * NYH + yh % NYH) * NC + core % NC


def dp_shift(dz, dyl):
    return [
        (dp_index(z, y), dp_index(z + dz, y + dyl)) for z in range(NZ) for y in range(NYL)
    ]


CORE_SWAP = [
    (mp_index(x, h, c), mp_index(x, h, c + 1))
    for x in range(NX)
    for h in range(NYH)
    for c in range(NC)
]
TRANSPOSE = [(d * 16 + m, m * 16 + d) for d in range(16) for m in range(16)]
SAME_CORE = [
    [mp_index(x, h, c) for x in range(NX) for h in range(NYH)] for c in range(NC)
]

CHUNKS = (
    ((0, 0), (0, 1), (1, 0), (-1, 0), (1, 1), (-1, 1), (2, 0), (-2, 0)),
    ((2, 1), (-2, 1), (3, 0), (-3, 0), (3, 1), (-3, 1), (4, 0), (4, 1)),
)


def dp_swap(z_bit, y_bit):
    return [
        (dp_index(z, y), dp_index(z ^ z_bit, y ^ y_bit)) for z in range(NZ) for y in range(NYL)
    ]


DP_SWAPS = tuple(dp_swap(*bits) for bits in ((0, 1), (1, 0), (2, 0), (4, 0)))


def exchange(x, axis, **kw):
    return lax.all_to_all(x, axis, 0, 0, tiled=True, **kw)


def share(x, count, axis, **kw):
    return exchange(jnp.tile(x, (count, 1)), axis, **kw)


def fence_kernel(*refs):
    del refs


def fence(*arrays, needs=()):
    anywhere = pl.BlockSpec(memory_space=pl.ANY)
    return pl.pallas_call(
        fence_kernel,
        out_shape=[jax.ShapeDtypeStruct(a.shape, a.dtype) for a in arrays],
        in_specs=[anywhere] * (len(arrays) + len(needs)),
        out_specs=[anywhere] * len(arrays),
        input_output_aliases={i: i for i in range(len(arrays))},
        compiler_params=pltpu.CompilerParams(vmem_limit_bytes=1024 * 1024),
    )(*arrays, *needs)


def up(x):
    return lax.ppermute(x, "dp", dp_shift(-1, 0))


def down(x):
    return lax.ppermute(x, "dp", dp_shift(1, 0))


def over(x):
    return lax.ppermute(x, "dp", dp_shift(0, 1))


def turn_kernel(count, core_ref, *refs):
    del core_ref
    blocks, basis_ref = refs[:count], refs[count]
    sib_ref, own_ref, tokens = refs[-3:]
    rows = blocks[0].shape[0]
    step = pl.program_id(0)

    @pl.when(step == 0)
    def _():
        for r, ref in enumerate(blocks):
            tokens[r * rows : (r + 1) * rows, :] = ref[...]
        sib_ref[...] = jnp.dot(
            tokens[...], basis_ref[...], preferred_element_type=jnp.float32
        ).astype(jnp.bfloat16)

    @pl.when(step == 1)
    def _():
        own_ref[...] = jnp.dot(
            tokens[...], basis_ref[...], preferred_element_type=jnp.float32
        )


def turn(core, blocks, basis, needs=()):
    rows, features = blocks[0].shape
    units = basis.shape[1] // 2
    tokens = rows * len(blocks)
    whole = lambda i, core_ref: (0, 0)
    side = lambda i, core_ref: (0, jnp.where(i == 0, 1 - core_ref[0], core_ref[0]))
    return pl.pallas_call(
        functools.partial(turn_kernel, len(blocks)),
        grid_spec=pltpu.PrefetchScalarGridSpec(
            num_scalar_prefetch=1,
            grid=(2,),
            in_specs=[pl.BlockSpec((rows, features), whole)] * len(blocks)
            + [pl.BlockSpec((features, units), side)]
            + [pl.BlockSpec(memory_space=pl.ANY)] * len(needs),
            out_specs=[pl.BlockSpec((tokens, units), whole)] * 2,
            scratch_shapes=[pltpu.VMEM((tokens, features), jnp.bfloat16)],
        ),
        out_shape=[
            jax.ShapeDtypeStruct((tokens, units), jnp.bfloat16),
            jax.ShapeDtypeStruct((tokens, units), jnp.float32),
        ],
        compiler_params=pltpu.CompilerParams(vmem_limit_bytes=56 * 1024 * 1024),
        cost_estimate=pl.CostEstimate(
            flops=2 * tokens * features * units * 2,
            bytes_accessed=2 * tokens * (features + 3 * units) + 4 * features * units,
            transcendentals=0,
        ),
    )(core.reshape(1), *blocks, basis, *needs)


def side_kernel(count, side_ref, *refs):
    del side_ref
    blocks, basis_ref = refs[:count], refs[count]
    out_ref, tokens, total = refs[-3:]
    rows = blocks[0].shape[0]
    depth = basis_ref.shape[0]
    step = pl.program_id(0)

    @pl.when(step == 0)
    def _():
        for r, ref in enumerate(blocks):
            tokens[r * rows : (r + 1) * rows, :] = ref[...]
        total[...] = jnp.dot(
            tokens[:, :depth], basis_ref[...], preferred_element_type=jnp.float32
        )

    @pl.when(step == 1)
    def _():
        out_ref[...] = (
            total[...]
            + jnp.dot(tokens[:, depth:], basis_ref[...], preferred_element_type=jnp.float32)
        ).astype(out_ref.dtype)


def turn_side(side, blocks, basis, kind, needs=()):
    rows, features = blocks[0].shape
    units = basis.shape[1] // 2
    tokens = rows * len(blocks)
    return pl.pallas_call(
        functools.partial(side_kernel, len(blocks)),
        grid_spec=pltpu.PrefetchScalarGridSpec(
            num_scalar_prefetch=1,
            grid=(2,),
            in_specs=[pl.BlockSpec((rows, features), lambda i, side_ref: (0, 0))] * len(blocks)
            + [pl.BlockSpec((features // 2, units), lambda i, side_ref: (i, side_ref[0]))]
            + [pl.BlockSpec(memory_space=pl.ANY)] * len(needs),
            out_specs=pl.BlockSpec((tokens, units), lambda i, side_ref: (0, 0)),
            scratch_shapes=[
                pltpu.VMEM((tokens, features), jnp.bfloat16),
                pltpu.VMEM((tokens, units), jnp.float32),
            ],
        ),
        out_shape=jax.ShapeDtypeStruct((tokens, units), kind),
        compiler_params=pltpu.CompilerParams(vmem_limit_bytes=56 * 1024 * 1024),
        cost_estimate=pl.CostEstimate(
            flops=2 * tokens * features * units,
            bytes_accessed=2 * tokens * (features + 2 * units) + 2 * features * units,
            transcendentals=0,
        ),
    )(side.reshape(1), *blocks, basis, *needs)


def after(x, y):
    return x + jnp.minimum(jnp.abs(y[:1, :1]), 0).astype(x.dtype)


def sum_kernel(parts_ref, *refs):
    out_ref = refs[-1]
    rows = parts_ref.shape[0] // CHIPS
    total = parts_ref[:rows, :].astype(jnp.float32)
    for i in range(1, CHIPS):
        total = total + parts_ref[i * rows : (i + 1) * rows, :].astype(jnp.float32)
    total = total.astype(jnp.bfloat16)
    for i in range(CHIPS):
        out_ref[i * rows : (i + 1) * rows, :] = total


def sum_and_copy(parts, *needs):
    vmem = pl.BlockSpec(memory_space=pltpu.VMEM)
    return pl.pallas_call(
        sum_kernel,
        out_shape=jax.ShapeDtypeStruct(parts.shape, jnp.bfloat16),
        in_specs=[vmem] + [pl.BlockSpec(memory_space=pl.ANY)] * len(needs),
        out_specs=vmem,
        compiler_params=pltpu.CompilerParams(vmem_limit_bytes=16 * 1024 * 1024),
        cost_estimate=pl.CostEstimate(
            flops=parts.size, bytes_accessed=parts.size * 4, transcendentals=0
        ),
    )(parts, *needs)


def score_kernel(acts_at_ref, place_ref, grads_hbm, own_acts_ref, sib_acts_ref, own_hbm,
                 sib_hbm, out_ref, train_grads, query_acts, train_acts, sums, grads_ref,
                 own_inv_ref, sib_inv_ref, arrived):
    rows = TQ + TS
    copies = [
        pltpu.make_async_copy(source, target, arrived.at[i])
        for i, (source, target) in enumerate(
            ((grads_hbm, grads_ref), (own_hbm, own_inv_ref), (sib_hbm, sib_inv_ref))
        )
    ]
    for copy in copies:
        copy.start()
    for r in range(GROUPS):
        for part, ref in ((0, own_acts_ref), (1, sib_acts_ref)):
            start = pl.multiple_of(acts_at_ref[r], rows)
            middle = pl.multiple_of(start + TQ, TQ)
            lanes = slice(part * 256, part * 256 + 256)
            query_acts[r * TQ : (r + 1) * TQ, lanes] = ref[pl.ds(start, TQ), :]
            train_acts[r * TS : (r + 1) * TS, lanes] = ref[pl.ds(middle, TS), :].astype(
                jnp.float32
            )
    copies[0].wait()
    for r in range(GROUPS):
        train_grads[r * TS : (r + 1) * TS, :] = grads_ref[r * rows + TQ : (r + 1) * rows, :]
    copies[1].wait()
    copies[2].wait()

    def one_query(n):
        grads = grads_ref[pl.ds(pl.multiple_of(n * rows, rows), TQ), :]
        total = jnp.zeros((GROUPS, 128), jnp.float32)
        for at, inv_ref in ((0, own_inv_ref), (256, sib_inv_ref)):
            acts = query_acts[pl.ds(pl.multiple_of(n * TQ, TQ), TQ), at : at + 256]
            gradient = lax.dot_general(
                grads, acts, (((0,), (0,)), ((), ())), preferred_element_type=jnp.float32
            )
            preconditioned = (gradient * inv_ref[...]).astype(jnp.bfloat16)
            projected = jnp.dot(
                train_grads[...], preconditioned, preferred_element_type=jnp.float32
            )
            terms = projected * train_acts[:, at : at + 256]
            terms = terms.reshape(GROUPS, TS, 256).sum(1)
            total = total + terms[:, :128] + terms[:, 128:]
        sums[pl.ds(n, 1)] = total[None]

    def four_queries(i, carry):
        for j in range(4):
            one_query(i * 4 + j)
        return carry

    lax.fori_loop(0, GROUPS // 4, four_queries, 0)
    scores = jnp.sum(sums[...], axis=2)
    hot = place_ref[...]
    scores = jnp.dot(
        hot, jnp.dot(scores, jnp.transpose(hot), precision=lax.Precision.HIGHEST),
        precision=lax.Precision.HIGHEST,
    )
    out_ref[...] = jnp.concatenate(
        [scores, jnp.zeros((GROUPS, 128 - GROUPS), jnp.float32)], 1
    )


def score_blocks(acts_at, place, grads, own_acts, sib_acts, own_inv, sib_inv):
    units, features = own_inv.shape
    vmem = pl.BlockSpec(memory_space=pltpu.VMEM)
    smem = pl.BlockSpec(memory_space=pltpu.SMEM)
    hbm = pl.BlockSpec(memory_space=pl.ANY)
    return pl.pallas_call(
        score_kernel,
        out_shape=jax.ShapeDtypeStruct((GROUPS, 128), jnp.float32),
        in_specs=[smem, vmem, hbm, vmem, vmem, hbm, hbm],
        out_specs=vmem,
        scratch_shapes=[
            pltpu.VMEM((GROUPS * TS, units), jnp.bfloat16),
            pltpu.VMEM((GROUPS * TQ, 2 * features), jnp.bfloat16),
            pltpu.VMEM((GROUPS * TS, 2 * features), jnp.float32),
            pltpu.VMEM((GROUPS, GROUPS, 128), jnp.float32),
            pltpu.VMEM(grads.shape, jnp.bfloat16),
            pltpu.VMEM((units, features), jnp.float32),
            pltpu.VMEM((units, features), jnp.float32),
            pltpu.SemaphoreType.DMA((3,)),
        ],
        compiler_params=pltpu.CompilerParams(vmem_limit_bytes=56 * 1024 * 1024),
        cost_estimate=pl.CostEstimate(
            flops=2 * GROUPS * units * 2 * features * (GROUPS * TS + TQ),
            bytes_accessed=8 * 1024 * 1024,
            transcendentals=0,
        ),
    )(acts_at, place, grads, own_acts, sib_acts, own_inv, sib_inv)


def shards(query_acts, query_grads, train_acts, train_grads, basis_in, basis_out, eigen):
    in_local = query_acts.shape[2]
    out_local = query_grads.shape[2]
    acts = jnp.concatenate([query_acts[0], train_acts[0]], 0)
    grads = jnp.concatenate([query_grads[0], train_grads[0]], 0)
    dp, mp = lax.axis_index("dp"), lax.axis_index("mp")
    z, yl, core = dp // NYL, dp % NYL, mp % NC
    units = out_local // 2
    rows = TQ + TS

    own_inv = 1.0 / (lax.dynamic_slice_in_dim(eigen, core * units, units, 0) + damping)
    sib_eigen = lax.ppermute(
        lax.dynamic_slice_in_dim(eigen, (1 - core) * units, units, 0), "mp", CORE_SWAP
    )
    sib_inv = 1.0 / (sib_eigen + damping)

    held = {(0, 0): grads}
    moved = lax.ppermute(acts, ("dp", "mp"), TRANSPOSE)
    held[(0, 0)], held[(1, 0)], held[(-1, 0)], held[(0, 1)] = fence(
        grads, up(grads), down(grads), over(grads)
    )
    held[(1, 0)], held[(-1, 0)], held[(2, 0)], held[(-2, 0)], held[(1, 1)] = fence(
        held[(1, 0)], held[(-1, 0)], up(held[(1, 0)]), down(held[(-1, 0)]),
        over(held[(1, 0)]),
    )
    (held[(2, 0)], held[(-2, 0)], held[(3, 0)], held[(-3, 0)], held[(1, 1)], held[(-1, 1)],
     moved) = fence(
        held[(2, 0)], held[(-2, 0)], up(held[(2, 0)]), down(held[(-2, 0)]), held[(1, 1)],
        over(held[(-1, 0)]), moved, needs=(own_inv, sib_inv),
    )
    every_acts = share(moved, GROUPS, "mp")
    held[(3, 0)], held[(-3, 0)], held[(2, 1)], held[(-2, 1)], held[(4, 0)], held[(3, 1)] = fence(
        held[(3, 0)], held[(-3, 0)], up(held[(1, 1)]), down(held[(-1, 1)]), down(held[(-3, 0)]),
        over(held[(3, 0)]),
    )
    held[(4, 1)], held[(-3, 1)] = up(held[(3, 1)]), over(held[(-3, 0)])

    summed = jnp.dot(every_acts, basis_in, preferred_element_type=jnp.float32)
    bits = (yl, z % 2, z // 2 % 2, z // 4)
    sums = []
    for k, (swap, bit) in enumerate(zip(DP_SWAPS, bits)):
        half = summed.shape[0] // 2
        away = lax.dynamic_slice_in_dim(summed, (1 - bit) * half, half, 0)
        mine = lax.dynamic_slice_in_dim(summed, bit * half, half, 0)
        if k == 0:
            first = away = away.astype(jnp.bfloat16)
        summed = mine + lax.ppermute(away, "dp", swap).astype(jnp.float32)
        sums.append(summed)
    own_acts = summed.astype(jnp.bfloat16)

    early, late = ([held[place] for place in chunk] for chunk in CHUNKS)
    sib_part, own_part = turn(core, early, basis_out, (held[(3, 1)],))
    got = lax.ppermute(sib_part, "mp", CORE_SWAP).astype(jnp.float32)
    early = (own_part + got).astype(jnp.bfloat16)
    sib_part = turn_side(1 - core, late, basis_out, jnp.bfloat16)
    got = lax.ppermute(sib_part, "mp", CORE_SWAP).astype(jnp.float32)
    own_part = turn_side(core, late, basis_out, jnp.float32, (first,))
    late = (own_part + after(got, sums[0])).astype(jnp.bfloat16)
    pairs = jnp.concatenate([early, late], 0)
    parts = exchange(pairs, "mp", axis_index_groups=SAME_CORE)
    copies = sum_and_copy(parts)

    own_acts = after(own_acts, copies)
    for swap in DP_SWAPS[::-1]:
        own_acts = jnp.concatenate([own_acts, lax.ppermute(own_acts, "dp", swap)], 0)
    sib_acts = lax.ppermute(own_acts, "mp", CORE_SWAP)

    all_grads = exchange(copies, "mp", axis_index_groups=SAME_CORE)

    places = [place for chunk in CHUNKS for place in chunk]
    dz = jnp.array([p[0] for p in places], jnp.int32)
    dy = jnp.array([p[1] for p in places], jnp.int32)
    order = ((z + dz + NZ) % NZ) * NYL + (yl + dy) % NYL
    place = (order[None, :] == jnp.arange(GROUPS, dtype=jnp.int32)[:, None]).astype(jnp.float32)

    kept = bits[0] * 8 + bits[1] * 4 + bits[2] * 2 + bits[3]
    acts_at = (order ^ kept) * rows

    scores = score_blocks(
        acts_at, place, all_grads, own_acts, sib_acts, own_inv, sib_inv
    )
    normalizer = float(TQ * TS * IN * OUT) ** (-0.5)
    scores = share(scores * normalizer, GROUPS, "mp").reshape(GROUPS, GROUPS, 128).sum(0)
    scores = share(scores, GROUPS, "dp").reshape(GROUPS, GROUPS, 128).sum(0)
    return scores[:, :GROUPS]


def solution(mesh):
    placed = (
        P("dp", None, "mp"),
        P("dp", None, "mp"),
        P("dp", None, "mp"),
        P("dp", None, "mp"),
        P("dp", "mp"),
        P("mp", "dp"),
        P("dp", "mp"),
    )
    return jax.shard_map(shards, mesh=mesh, in_specs=placed, out_specs=P(), check_vma=False)
```
